1024 devices in a mesh: rows: 128 (over z, x), rep: 8 (over y, core).
Axes of the slice: x: 4, y: 4, z: 32, core: 2. Of those that a mesh axis runs over, the one named last changes fastest.
Arguments:
- features: bfloat16 [262144, 1024], P('rows', 'rep'), may hold values from -6 to 6
- tile_rows: int32 [128, 4, 16], P('rows'), may hold values from 0 to 15
- tile_cols: int32 [128, 4, 16], P('rows'), may hold values from 0 to 15
- tile_counts: int32 [128, 4], P('rows'), may hold values from 1 to 16, as said below
- tile_values: bfloat16 [128, 4, 16, 128, 128], P('rows'), may hold values from 0 to 0.099609375
- weight: bfloat16 [1024, 1024], P(None, 'rep'), may hold values from -0.1875 to 0.1875
Outputs:
- activated: bfloat16 [262144, 1024], P(('rows', 'rep'))
The draws below stay inside these ranges and needn't reach their ends.
Inputs may be any that keep to these rules, and one draw needn't show every extreme that they name: `tile_counts`: some row group has all 16 slots live for some owner in every draw.
All inputs are finite; a program needn't handle non-finite values.
Results may differ from the reference program's by a relative error of at most 0.0049.
Values may be sent and summed in bfloat16 or wider, within the bound.
A program may use at most 32 MiB of HBM per device.

```python
import jax
import jax.numpy as jnp
from jax import lax

F = 1024
TILE = 128
SECTIONS = 4
SLOTS = 16
ROWS_DEV = 2048
BLOCKS = 128
NODES = 262144
N_ROWS = 128


def draw_tile_counts(key, part):
    key = jax.random.fold_in(key, 7)
    first, second = jax.random.split(key)
    counts = jax.random.randint(first, (BLOCKS * SECTIONS,), 1, SLOTS + 1)
    chosen = jax.random.randint(second, (), 0, BLOCKS * SECTIONS)
    places = jnp.arange(BLOCKS * SECTIONS, dtype=jnp.int32)
    counts = jnp.where(places == chosen, SLOTS, counts)
    return counts.reshape(BLOCKS, SECTIONS).astype(jnp.int32)


def touch_ends(drawn, rng, least, largest):
    place = [jax.random.randint(jax.random.fold_in(rng, axis), (), 0, length) for axis, length in enumerate(drawn.shape)]
    widest = drawn.shape.index(max(drawn.shape))
    neighbour = place[:widest] + [(place[widest] + 1) % drawn.shape[widest]] + place[widest + 1:]
    return drawn.at[tuple(place)].set(least).at[tuple(neighbour)].set(largest)


def block_levels(own_key, dims, pieces, least, largest):
    def one(dim, blocks):
        draws = jax.random.uniform(jax.random.fold_in(jax.random.fold_in(own_key, 6), dim), (blocks,), jnp.float32, least / len(pieces), largest / len(pieces))
        return jnp.repeat(jnp.exp(draws), dims[dim] // blocks).reshape((-1,) + (1,) * (len(dims) - dim - 1))

    loudness = one(*pieces[0])
    for cut in pieces[1:]:
        loudness = loudness * one(*cut)
    return loudness


def gaussian(rng, extent, scale, bound, pieces=(), held_as=jnp.bfloat16):
    values = jax.random.normal(rng, extent, jnp.float32) * scale
    if len(pieces) > 0:
        values = block_levels(rng, extent, pieces, -0.22, 0.18) * values
    return jnp.clip(values, min=-bound, max=bound).astype(held_as)


def setup_inputs(seed: int = 0) -> dict:
    arg_keys = jax.random.split(jax.random.key(seed), 7)
    return {
        "features": gaussian(arg_keys[0], (NODES, F), 1.0, 6.0, ((0, 128), (1, 8))),
        "tile_rows": touch_ends(jax.random.randint(arg_keys[1], (BLOCKS, SECTIONS, SLOTS), 0, ROWS_DEV // TILE), jax.random.fold_in(arg_keys[1], 1), 0, (ROWS_DEV // TILE) - 1).astype(jnp.int32),
        "tile_cols": touch_ends(jax.random.randint(arg_keys[2], (BLOCKS, SECTIONS, SLOTS), 0, ROWS_DEV // TILE), jax.random.fold_in(arg_keys[2], 1), 0, (ROWS_DEV // TILE) - 1).astype(jnp.int32),
        "tile_counts": draw_tile_counts(jax.random.fold_in(arg_keys[6], 71), 0),
        "tile_values": jnp.clip(0.099609375 * jax.random.uniform(arg_keys[4], (BLOCKS, SECTIONS, SLOTS, TILE, TILE), jnp.float32) ** block_levels(arg_keys[4], (BLOCKS, SECTIONS, SLOTS, TILE, TILE), ((0, 128),), -0.2, 0.2), 0.0, 0.099609375).astype(jnp.bfloat16),
        "weight": gaussian(arg_keys[5], (F, F), F ** -0.5, 0.1875, ((1, 8),)),
    }


def reference(features, tile_rows, tile_cols, tile_counts, tile_values, weight):
    row_tiles = ROWS_DEV // TILE
    owners = [section * (N_ROWS // SECTIONS) for section in range(SECTIONS)]
    panels = jnp.stack([features[owner * ROWS_DEV:(owner + 1) * ROWS_DEV] for owner in owners])
    panels = panels.reshape(SECTIONS, row_tiles, TILE, F)
    section_ids = jnp.arange(SECTIONS, dtype=jnp.int32)[:, None]

    def one_group(items):
        rows_here, cols_here, counts_here, values_here = items
        picked = panels[section_ids, cols_here]
        products = jnp.einsum("asij,asjk->asik", values_here.astype(jnp.float32), picked.astype(jnp.float32),
                              precision=lax.Precision.HIGHEST)
        live = jnp.arange(SLOTS, dtype=jnp.int32)[None, :] < counts_here[:, None]
        products = jnp.where(live[:, :, None, None], products, jnp.float32(0.0))
        total = jnp.zeros((row_tiles, TILE, F), jnp.float32)
        total = total.at[rows_here.reshape(-1)].add(products.reshape(SECTIONS * SLOTS, TILE, F))
        aggregate = total.reshape(ROWS_DEV, F).astype(jnp.bfloat16)
        mixed = jnp.dot(aggregate, weight, preferred_element_type=jnp.float32)
        return jnp.maximum(mixed, 0.0).astype(jnp.bfloat16)

    result = lax.map(one_group, (tile_rows, tile_cols, tile_counts, tile_values))
    return result.reshape(N_ROWS * ROWS_DEV, F)
```

```python
import jax
import jax.numpy as jnp
from jax import lax
from jax.experimental import pallas as pl
from jax.experimental.pallas import tpu as pltpu
from jax.sharding import PartitionSpec as P

MESH = pl.DeviceIdType.MESH
ZS, XS, REPS = 32, 4, 8
SECTIONS, SLOTS, TILE = 4, 16, 128
GAP = ZS // SECTIONS
HALF = ZS // 2
GROUP = 4 * TILE


def kernel(
    rows_ref, cols_ref, counts_ref, feat_ref, tiles_ref, weight_ref, out_ref,
    panel, whole, tiles, weights, sums, block_out, block_in, prev, last,
    local_sem, recv_sem, send_sem, wsend_sem, wrecv_sem, bsend_sem, brecv_sem,
):
    me, rep = lax.axis_index("rows"), lax.axis_index("rep")
    z, x = me // XS, me % XS

    def at(dz, dx):
        return (((z + dz + ZS) % ZS) * XS + (x + dx + XS) % XS, rep)

    def other(i):
        return lax.rem(rep + i, REPS)

    is_owner = jnp.logical_and(x == 0, z % GAP == 0)
    mine = z // GAP

    barrier = pltpu.get_barrier_semaphore()
    partners = [at(d, 0) for d in (1, -1, 2, -2, 3, -3, 4, -4)] + [at(0, d) for d in (1, -1, 2)]
    for partner in partners:
        pl.semaphore_signal(barrier, inc=1, device_id=partner, device_id_type=MESH)
    for i in range(1, REPS):
        pl.semaphore_signal(barrier, inc=1, device_id=(me, other(i)), device_id_type=MESH)

    own_panel = pltpu.make_async_copy(feat_ref, panel.at[mine], local_sem.at[0])
    own_weight = pltpu.make_async_copy(weight_ref, weights.at[rep], local_sem.at[1])
    own_tiles = pltpu.make_async_copy(tiles_ref.at[0], tiles, local_sem.at[2])

    @pl.when(is_owner)
    def _():
        own_panel.start()

    own_tiles.start()
    own_weight.start()
    sums[SECTIONS * SLOTS] = jnp.zeros((TILE, TILE), jnp.float32)

    def along(section):
        dz = lax.rem(z - GAP * section + ZS, ZS)
        far = jnp.where(dz <= HALF, dz, ZS - dz)
        return dz, (far + 3) // 4

    for t in range(16):
        last[t] = SECTIONS * SLOTS

    def link(step, carry):
        def of(section, carry):
            _, turn = along(section)

            @pl.when(turn == step)
            def _():
                def slot(j, carry):
                    row = rows_ref[0, section, j]
                    here = section * SLOTS + j
                    prev[here] = last[row]
                    row = jnp.where(j < counts_ref[0, section], row, 16)
                    for t in range(16):
                        last[t] = jnp.where(row == t, here, last[t])
                    return carry

                lax.fori_loop(0, SLOTS, slot, 0)

            return carry

        return lax.fori_loop(0, SECTIONS, of, carry)

    lax.fori_loop(0, 5, link, 0)

    pl.semaphore_wait(barrier, len(partners) + REPS - 1)

    def wcopy(i):
        return pltpu.make_async_remote_copy(
            weight_ref, weights.at[rep], wsend_sem.at[i], wrecv_sem.at[rep],
            device_id=(me, other(i)), device_id_type=MESH)

    def rows_of(section, tile, count=1):
        return panel.at[section, pl.ds(tile, count)]

    def copy(section, tile, count, send, recv, to):
        ref = rows_of(section, tile, count)
        return pltpu.make_async_remote_copy(
            ref, ref, send_sem.at[section, send], recv_sem.at[section, recv], device_id=to, device_id_type=MESH)

    def sends_spread(section, act, wait):
        dz, _ = along(section)
        in_row = dz == 0

        @pl.when(in_row)
        def _():
            for b in range(4):
                @pl.when(x == 0)
                def _():
                    for i, dx in enumerate((2, 1, 3)):
                        act(copy(section, 4 * dx + b, 1, 3 * b + i, b, at(0, dx)))

                if wait:
                    @pl.when(x != 0)
                    def _():
                        copy(section, 4 * x + b, 1, 0, b, at(0, 1)).wait_recv()

                act(copy(section, 4 * x + b, 1, 12 + 2 * b, 0, at(b if b else 4, 0)))
                act(copy(section, 4 * x + b, 1, 13 + 2 * b, 0, at(b - 4, 0)))

        own = 4 * x + z % 4

        @pl.when(jnp.logical_not(in_row))
        def _():
            if wait:
                copy(section, own, 1, 0, 0, at(1, 0)).wait_recv()

            @pl.when(dz + 4 <= HALF)
            def _():
                act(copy(section, own, 1, 12, 0, at(4, 0)))

            @pl.when(dz - 4 > HALF)
            def _():
                act(copy(section, own, 1, 12, 0, at(-4, 0)))

        skip = 2 - 4 * (section % 2)

        @pl.when(dz + 1 != ZS)
        def _():
            act(copy(section, own, 1, 20, 4, at(1, 0)))

        @pl.when(dz != 1)
        def _():
            act(copy(section, own, 1, 21, 5, at(-1, 0)))

        @pl.when(lax.rem(dz + skip + ZS, ZS) != 0)
        def _():
            act(copy(section, own, 1, 22, 6, at(skip, 0)))

    def sends_across(section, act, wait):
        dz, _ = along(section)
        if wait:
            @pl.when(dz != 0)
            def _():
                copy(section, 4 * x + (z + 3) % 4, 1, 0, 4, at(1, 0)).wait_recv()
                copy(section, 4 * x + (z + 1) % 4, 1, 0, 5, at(1, 0)).wait_recv()
                copy(section, 4 * x + (z + 2) % 4, 1, 0, 6, at(1, 0)).wait_recv()

        @pl.when(jnp.logical_or(dz != 0, x != 3))
        def _():
            act(copy(section, 4 * x, 4, 23, 7, at(0, 1)))

        @pl.when(jnp.logical_or(dz != 0, x != 1))
        def _():
            act(copy(section, 4 * x, 4, 24, 8, at(0, -1)))

    def sends_on(section, act, wait):
        dz, _ = along(section)
        left, right = (x + 3) % 4, (x + 1) % 4
        gets = jnp.logical_or(dz != 0, x != 0)
        if wait:
            @pl.when(gets)
            def _():
                copy(section, 4 * left, 4, 0, 7, at(0, 1)).wait_recv()

        @pl.when(jnp.logical_or(dz != 0, x != 3))
        def _():
            act(copy(section, 4 * left, 2, 25, 9, at(0, 1)))

        if wait:
            @pl.when(gets)
            def _():
                copy(section, 4 * right, 4, 0, 8, at(0, 1)).wait_recv()

        @pl.when(jnp.logical_or(dz != 0, x != 1))
        def _():
            act(copy(section, 4 * right + 2, 2, 26, 10, at(0, -1)))

    def products(section):
        dz, _ = along(section)

        @pl.when(jnp.logical_or(dz != 0, x != 0))
        def _():
            facing = (x + 2) % 4
            copy(section, 4 * facing, 2, 0, 9, at(0, 1)).wait_recv()
            copy(section, 4 * facing + 2, 2, 0, 10, at(0, 1)).wait_recv()

        whole[...] = panel[section]
        for j in range(SLOTS):
            here = section * SLOTS + j
            sums[here] = sums[prev[here]] + jnp.dot(
                tiles[section, j], whole[cols_ref[0, section, j]], preferred_element_type=jnp.float32)

    def start(c):
        c.start()

    def step(now, carry):
        def for_each(turn, what):
            def of(section, carry):
                _, first = along(section)

                @pl.when(first == turn)
                def _():
                    what(section)

                return carry

            lax.fori_loop(0, SECTIONS, of, 0)

        for_each(now, lambda s: sends_spread(s, start, True))

        @pl.when(now == 0)
        def _():
            def one(i, carry):
                wcopy(i).start()
                return carry

            lax.fori_loop(1, REPS, one, 0)

        for_each(now - 1, lambda s: sends_across(s, start, True))
        for_each(now - 2, lambda s: sends_on(s, start, True))
        for_each(now - 3, products)
        return carry

    @pl.when(is_owner)
    def _():
        own_panel.wait()

    own_tiles.wait()
    own_weight.wait()
    lax.fori_loop(0, 8, step, 0)

    def bcopy(i):
        to = other(i)
        return pltpu.make_async_remote_copy(
            block_out.at[to], block_in.at[rep], bsend_sem.at[i], brecv_sem.at[rep],
            device_id=(me, to), device_id_type=MESH)

    def send_block(i, carry):
        to = other(i)
        for half in range(2):
            block_out[to, pl.ds(half * TILE, TILE), :] = sums[last[2 * to + half]].astype(jnp.bfloat16)

        bcopy(i).start()
        return carry

    lax.fori_loop(1, REPS, send_block, 0)
    for half in range(2):
        block_in[rep, pl.ds(half * TILE, TILE), :] = sums[last[2 * rep + half]].astype(jnp.bfloat16)

    def arrived(i, carry):
        source = other(i)
        pltpu.make_async_remote_copy(
            weight_ref, weights.at[source], wsend_sem.at[i], wrecv_sem.at[source],
            device_id=(me, source), device_id_type=MESH).wait_recv()
        pltpu.make_async_remote_copy(
            block_out.at[source], block_in.at[source], bsend_sem.at[i], brecv_sem.at[source],
            device_id=(me, source), device_id_type=MESH).wait_recv()
        return carry

    lax.fori_loop(1, REPS, arrived, 0)

    left = jnp.concatenate([block_in[i] for i in range(REPS)], axis=1)
    for q in range(REPS // 2):
        right = jnp.concatenate([weights[2 * q], weights[2 * q + 1]], axis=1)
        mixed = jnp.dot(left, right, preferred_element_type=jnp.float32)
        out_ref[:, pl.ds(2 * q * TILE, 2 * TILE)] = jnp.maximum(mixed, 0.0).astype(jnp.bfloat16)

    def finish(section, carry):
        def done(c):
            c.wait_send()

        sends_spread(section, done, False)
        sends_across(section, done, False)
        sends_on(section, done, False)
        return carry

    lax.fori_loop(0, SECTIONS, finish, 0)

    def sent(i, carry):
        wcopy(i).wait_send()
        bcopy(i).wait_send()
        return carry

    lax.fori_loop(1, REPS, sent, 0)


def shards(features, tile_rows, tile_cols, tile_counts, tile_values, weight):
    height, width = features.shape
    smem = pl.BlockSpec(memory_space=pltpu.SMEM)
    hbm = pl.BlockSpec(memory_space=pl.ANY)
    dma = pltpu.SemaphoreType.DMA
    return pl.pallas_call(
        kernel,
        out_shape=jax.ShapeDtypeStruct((height // REPS, width * REPS), jnp.bfloat16),
        in_specs=[smem, smem, smem, hbm, hbm, hbm],
        out_specs=pl.BlockSpec(memory_space=pltpu.VMEM),
        scratch_shapes=[
            pltpu.VMEM((SECTIONS, 16, TILE, width), jnp.bfloat16),
            pltpu.VMEM((16, TILE, width), jnp.bfloat16),
            pltpu.VMEM((SECTIONS, SLOTS, TILE, TILE), jnp.bfloat16),
            pltpu.VMEM((REPS, weight.shape[0], weight.shape[1]), jnp.bfloat16),
            pltpu.VMEM((SECTIONS * SLOTS + 1, TILE, TILE), jnp.float32),
            pltpu.VMEM((REPS, height // REPS, width), jnp.bfloat16),
            pltpu.VMEM((REPS, height // REPS, width), jnp.bfloat16),
            pltpu.SMEM((SECTIONS * SLOTS,), jnp.int32),
            pltpu.SMEM((16,), jnp.int32),
            dma((3,)),
            dma((SECTIONS, 11)),
            dma((SECTIONS, 27)),
            dma((REPS,)),
            dma((REPS,)),
            dma((REPS,)),
            dma((REPS,)),
        ],
        compiler_params=pltpu.CompilerParams(
            collective_id=0, has_side_effects=True, vmem_limit_bytes=60 << 20
        ),
        cost_estimate=pl.CostEstimate(flops=1_610_612_736, bytes_accessed=8_000_000, transcendentals=0),
        name="layer",
    )(tile_rows, tile_cols, tile_counts, features.reshape(16, TILE, width), tile_values, weight)


def solution(mesh):
    return jax.shard_map(
        shards,
        mesh=mesh,
        in_specs=(
            P("rows", "rep"),
            P("rows", None, None),
            P("rows", None, None),
            P("rows", None),
            P("rows", None, None, None, None),
            P(None, "rep"),
        ),
        out_specs=P(("rows", "rep"), None),
        check_vma=False,
    )
```

```python
import jax
import jax.numpy as jnp
from jax import lax
from jax.experimental import pallas as pl
from jax.experimental.pallas import tpu as pltpu
from jax.sharding import PartitionSpec as P

MESH = pl.DeviceIdType.MESH
ZS, XS, REPS = 32, 4, 8
SECTIONS, SLOTS, TILE = 4, 16, 128
GAP = ZS // SECTIONS
HALF = ZS // 2
HOP = 4
NONE = SECTIONS * SLOTS
OUT = pltpu.VMEM


def kernel(
    rows_hbm, cols_hbm, counts_hbm, feat_ref, tiles_ref, weight_ref, out_ref,
    panel, whole, tiles, weights, sums, block_out, block_in, rows_ref, cols_ref, counts_ref, prev, last,
    local_sem, recv_sem, send_sem, wsend_sem, wrecv_sem, bsend_sem, brecv_sem,
):
    me, rep = lax.axis_index("rows"), lax.axis_index("rep")
    z, x = me // XS, me % XS
    past = z % GAP

    def at(dz, dx):
        return (((z + dz + ZS) % ZS) * XS + (x + dx + XS) % XS, rep)

    def other(i):
        far, turn = 3 - (i - 1) // 2, 1 - (i - 1) % 2
        return 2 * ((rep // 2 + far) % 4) + (rep + turn) % 2

    is_owner = jnp.logical_and(x == 0, past == 0)

    barrier = pltpu.get_barrier_semaphore()

    def greet(to):
        pl.semaphore_signal(barrier, inc=1, device_id=to, device_id_type=MESH)

    for d in range(HOP, 0, -1):
        greet(at(d, 0))
        greet(at(-d, 0))

    greet(at(0, 1))
    greet(at(0, -1))

    @pl.when(jnp.logical_and(past == 0, x == 2))
    def _():
        greet(at(0, -2))

    for i in range(1, REPS):
        greet((me, other(i)))

    own_panel = pltpu.make_async_copy(feat_ref, panel.at[z // GAP], local_sem.at[0])
    own_weight = pltpu.make_async_copy(weight_ref, weights.at[rep], local_sem.at[1])
    own_tiles = pltpu.make_async_copy(tiles_ref.at[0], tiles, local_sem.at[2])
    lists = [
        pltpu.make_async_copy(rows_hbm, rows_ref, local_sem.at[3]),
        pltpu.make_async_copy(cols_hbm, cols_ref, local_sem.at[4]),
        pltpu.make_async_copy(counts_hbm, counts_ref, local_sem.at[5]),
    ]

    @pl.when(is_owner)
    def _():
        own_panel.start()

    for c in lists + [own_tiles, own_weight]:
        c.start()
    sums[NONE] = jnp.zeros((TILE, TILE), jnp.float32)

    def along(section):
        dz = lax.rem(z - GAP * section + ZS, ZS)
        far = jnp.where(dz <= HALF, dz, ZS - dz)
        return dz, (far + HOP - 1) // HOP

    def make_links():
        for c in lists:
            c.wait()
        keys = [along(s)[1] * SECTIONS + s for s in range(SECTIONS)]
        ranks = [sum((other < key).astype(jnp.int32) for other in keys) for key in keys]
        order = [sum(jnp.where(rank == k, s, 0) for s, rank in enumerate(ranks)) for k in range(SECTIONS)]

        def slot(i, ends):
            k, j = i // SLOTS, i % SLOTS
            section = sum(jnp.where(k == n, s, 0) for n, s in enumerate(order))
            row = jnp.where(j < counts_ref[0, section], rows_ref[0, section, j], 16)
            here = section * SLOTS + j
            before = jnp.int32(NONE)
            after = []
            for t in range(16):
                same = row == t
                before = jnp.where(same, ends[t], before)
                after.append(jnp.where(same, here, ends[t]))
            prev[here] = before
            return tuple(after)

        ends = lax.fori_loop(0, NONE, slot, (jnp.int32(NONE),) * 16)
        for t in range(16):
            last[t] = ends[t]

    def wcopy(i):
        return pltpu.make_async_remote_copy(
            weight_ref, weights.at[rep], wsend_sem.at[i], wrecv_sem.at[rep],
            device_id=(me, other(i)), device_id_type=MESH)

    def copy(section, group, b, send, recv, to, count=1):
        ref = panel.at[section, pl.ds(4 * group + b, count)]
        return pltpu.make_async_remote_copy(
            ref, ref, send_sem.at[section, send], recv_sem.at[section, recv], device_id=to, device_id_type=MESH)

    def gets(section):
        dz, _ = along(section)
        return jnp.logical_or(dz != 0, x != 0)

    def spread(section, act, wait):
        dz, _ = along(section)
        in_row = dz == 0

        @pl.when(in_row)
        def _():
            @pl.when(x == 0)
            def _():
                for b in (0, 3, 1, 2):
                    for i, dx in enumerate((2, 1, 3)):
                        act(copy(section, dx, b, 3 * b + i, b, at(0, dx)))

            needs = {4: (0,), 3: (3, 1), 2: (2,)}
            for d in range(HOP, 0, -1):
                if wait and d in needs:
                    @pl.when(x != 0)
                    def _():
                        for b in needs[d]:
                            copy(section, x, b, 0, b, at(0, 1)).wait_recv()

                act(copy(section, x, d % 4, 10 + 2 * d, 0, at(d, 0)))
                act(copy(section, x, -d % 4, 11 + 2 * d, 0, at(-d, 0)))

        own = z % 4

        @pl.when(jnp.logical_not(in_row))
        def _():
            if wait:
                copy(section, x, own, 0, 0, at(1, 0)).wait_recv()

            @pl.when(dz <= HALF - HOP)
            def _():
                act(copy(section, x, own, 12, 0, at(HOP, 0)))

            @pl.when(dz > HALF + HOP)
            def _():
                act(copy(section, x, own, 12, 0, at(-HOP, 0)))

        out = dz <= HALF
        far = jnp.where(out, dz, ZS - dz)
        place = (far + 3) % 4
        for i in range(1, 4):
            step = (place + i) % 4 - place

            @pl.when(jnp.logical_and(far > 0, jnp.logical_or(out, far + step != HALF)))
            def _():
                act(copy(section, x, own, 27 + i, 4 + own, at(jnp.where(out, step, -step), 0)))

        @pl.when(dz == HALF)
        def _():
            for i in range(1, 4):
                act(copy(section, x, own, 30 + i, 4 + own, at(i, 0)))

    def across(section, act, wait):
        dz, _ = along(section)
        if wait:
            @pl.when(dz != 0)
            def _():
                for step in (1, 2, 3):
                    b = (z + step) % 4
                    copy(section, x, b, 0, 4 + b, at(1, 0)).wait_recv()

        for first, right, left in ((True, 0, 2), (False, 2, 0)):
            @pl.when(jnp.logical_or(dz != 0, x != 3))
            def _():
                act(copy(section, x, right, 34 if first else 38, 8 if first else 12, at(0, 1), 2))

            @pl.when(jnp.logical_or(dz != 0, x != 1))
            def _():
                act(copy(section, x, left, 35 if first else 39, 9 if first else 13, at(0, -1), 2))

    def onward(section, act, wait):
        dz, _ = along(section)
        left, right = (x + 3) % 4, (x + 1) % 4
        if wait:
            @pl.when(gets(section))
            def _():
                copy(section, left, 0, 0, 8, at(0, 1), 2).wait_recv()

        @pl.when(jnp.logical_or(dz != 0, x != 3))
        def _():
            act(copy(section, left, 0, 36, 10, at(0, 1), 2))

        if wait:
            @pl.when(gets(section))
            def _():
                copy(section, right, 2, 0, 9, at(0, 1), 2).wait_recv()

        @pl.when(jnp.logical_or(dz != 0, x != 1))
        def _():
            act(copy(section, right, 2, 37, 11, at(0, -1), 2))

    def complete(section):
        @pl.when(gets(section))
        def _():
            facing = (x + 2) % 4
            copy(section, (x + 3) % 4, 2, 0, 12, at(0, 1), 2).wait_recv()
            copy(section, (x + 1) % 4, 0, 0, 13, at(0, 1), 2).wait_recv()
            copy(section, facing, 0, 0, 10, at(0, 1), 2).wait_recv()
            copy(section, facing, 2, 0, 11, at(0, 1), 2).wait_recv()

    def products(section):
        complete(section)
        whole[...] = panel[section]
        for j in range(SLOTS):
            here = section * SLOTS + j
            sums[here] = sums[prev[here]] + jnp.dot(
                tiles[section, j], whole[cols_ref[0, section, j]], preferred_element_type=jnp.float32)

    def start(c):
        c.start()

    def step(now, carry):
        def for_each(turn, what):
            def of(section, carry):
                _, first = along(section)

                @pl.when(first == turn)
                def _():
                    what(section)

                return carry

            lax.fori_loop(0, SECTIONS, of, 0)

        for_each(now, lambda s: spread(s, start, True))

        @pl.when(now == 0)
        def _():
            def one(i, carry):
                wcopy(i).start()
                return carry

            lax.fori_loop(1, REPS, one, 0)
            make_links()
            own_tiles.wait()

        for_each(now - 1, lambda s: across(s, start, True))
        for_each(now - 2, lambda s: onward(s, start, True))
        for_each(now - 3, products)
        return carry

    pl.semaphore_wait(barrier, jnp.where(is_owner, 18, 17))

    @pl.when(is_owner)
    def _():
        own_panel.wait()

    lax.fori_loop(0, 8, step, 0)

    def bcopy(i):
        to = other(i)
        return pltpu.make_async_remote_copy(
            block_out.at[to], block_in.at[rep], bsend_sem.at[i], brecv_sem.at[rep],
            device_id=(me, to), device_id_type=MESH)

    def send_block(i, carry):
        to = other(i)
        for half in range(2):
            block_out[to, pl.ds(half * TILE, TILE), :] = sums[last[2 * to + half]].astype(jnp.bfloat16)

        bcopy(i).start()
        return carry

    lax.fori_loop(1, REPS, send_block, 0)
    for half in range(2):
        block_in[rep, pl.ds(half * TILE, TILE), :] = sums[last[2 * rep + half]].astype(jnp.bfloat16)

    own_weight.wait()

    def arrived(i, carry):
        source = other(i)
        pltpu.make_async_remote_copy(
            weight_ref, weights.at[source], wsend_sem.at[i], wrecv_sem.at[source],
            device_id=(me, source), device_id_type=MESH).wait_recv()
        pltpu.make_async_remote_copy(
            block_out.at[source], block_in.at[source], bsend_sem.at[i], brecv_sem.at[source],
            device_id=(me, source), device_id_type=MESH).wait_recv()
        return carry

    lax.fori_loop(1, REPS, arrived, 0)

    left = jnp.concatenate([block_in[i] for i in range(REPS)], axis=1)
    for q in range(REPS // 2):
        right = jnp.concatenate([weights[2 * q], weights[2 * q + 1]], axis=1)
        mixed = jnp.dot(left, right, preferred_element_type=jnp.float32)
        out_ref[:, pl.ds(2 * q * TILE, 2 * TILE)] = jnp.maximum(mixed, 0.0).astype(jnp.bfloat16)

    def finish(section, carry):
        def done(c):
            c.wait_send()

        spread(section, done, False)
        across(section, done, False)
        onward(section, done, False)
        return carry

    lax.fori_loop(0, SECTIONS, finish, 0)

    def sent(i, carry):
        wcopy(i).wait_send()
        bcopy(i).wait_send()
        return carry

    lax.fori_loop(1, REPS, sent, 0)


def shards(features, tile_rows, tile_cols, tile_counts, tile_values, weight):
    height, width = features.shape
    hbm = pl.BlockSpec(memory_space=pl.ANY)
    dma = pltpu.SemaphoreType.DMA
    return pl.pallas_call(
        kernel,
        out_shape=OUT((height // REPS, width * REPS), jnp.bfloat16),
        in_specs=[hbm] * 6,
        out_specs=pl.BlockSpec(memory_space=pltpu.VMEM),
        scratch_shapes=[
            pltpu.VMEM((SECTIONS, 16, TILE, width), jnp.bfloat16),
            pltpu.VMEM((16, TILE, width), jnp.bfloat16),
            pltpu.VMEM((SECTIONS, SLOTS, TILE, TILE), jnp.bfloat16),
            pltpu.VMEM((REPS, weight.shape[0], weight.shape[1]), jnp.bfloat16),
            pltpu.VMEM((SECTIONS * SLOTS + 1, TILE, TILE), jnp.float32),
            pltpu.VMEM((REPS, height // REPS, width), jnp.bfloat16),
            pltpu.VMEM((REPS, height // REPS, width), jnp.bfloat16),
            pltpu.SMEM(tile_rows.shape, jnp.int32),
            pltpu.SMEM(tile_cols.shape, jnp.int32),
            pltpu.SMEM(tile_counts.shape, jnp.int32),
            pltpu.SMEM((SECTIONS * SLOTS,), jnp.int32),
            pltpu.SMEM((16,), jnp.int32),
            dma((6,)),
            dma((SECTIONS, 14)),
            dma((SECTIONS, 40)),
            dma((REPS,)),
            dma((REPS,)),
            dma((REPS,)),
            dma((REPS,)),
        ],
        compiler_params=pltpu.CompilerParams(
            collective_id=0, has_side_effects=True, vmem_limit_bytes=60 << 20
        ),
        cost_estimate=pl.CostEstimate(flops=1_610_612_736, bytes_accessed=8_000_000, transcendentals=0),
        name="layer",
    )(tile_rows, tile_cols, tile_counts, features.reshape(16, TILE, width), tile_values, weight)


def solution(mesh):
    return jax.shard_map(
        shards,
        mesh=mesh,
        in_specs=(
            P("rows", "rep"),
            P("rows", None, None),
            P("rows", None, None),
            P("rows", None),
            P("rows", None, None, None, None),
            P(None, "rep"),
        ),
        out_specs=P(("rows", "rep"), None),
        check_vma=False,
    )
```

```python
import jax
import jax.numpy as jnp
from jax import lax
from jax.experimental import pallas as pl
from jax.experimental.pallas import tpu as pltpu
from jax.sharding import PartitionSpec as P

MESH = pl.DeviceIdType.MESH
ZS, XS, REPS = 32, 4, 8
SECTIONS, SLOTS, TILE = 4, 16, 128
GAP = ZS // SECTIONS
HALF = ZS // 2
HOP = 4
NONE = SECTIONS * SLOTS
OUT = pltpu.VMEM


def kernel(
    rows_hbm, cols_hbm, counts_hbm, feat_ref, tiles_ref, weight_ref, out_ref,
    panel, whole, tiles, weights, sums, block_out, block_in, rows_ref, cols_ref, counts_ref, prev, last,
    local_sem, recv_sem, send_sem, wsend_sem, wrecv_sem, bsend_sem, brecv_sem,
):
    me, rep = lax.axis_index("rows"), lax.axis_index("rep")
    z, x = me // XS, me % XS
    past = z % GAP

    def at(dz, dx):
        return (((z + dz + ZS) % ZS) * XS + (x + dx + XS) % XS, rep)

    def other(i):
        far, turn = 3 - (i - 1) // 2, 1 - (i - 1) % 2
        return 2 * ((rep // 2 + far) % 4) + (rep + turn) % 2

    is_owner = jnp.logical_and(x == 0, past == 0)

    barrier = pltpu.get_barrier_semaphore()

    def greet(to):
        pl.semaphore_signal(barrier, inc=1, device_id=to, device_id_type=MESH)

    for d in range(HOP, 0, -1):
        greet(at(d, 0))
        greet(at(-d, 0))

    greet(at(0, 1))
    greet(at(0, -1))

    @pl.when(jnp.logical_and(past == 0, x == 2))
    def _():
        greet(at(0, -2))

    for i in range(1, REPS):
        greet((me, other(i)))

    own_panel = pltpu.make_async_copy(feat_ref, panel.at[z // GAP], local_sem.at[0])
    own_weight = pltpu.make_async_copy(weight_ref, weights.at[rep], local_sem.at[1])
    own_tiles = pltpu.make_async_copy(tiles_ref.at[0], tiles, local_sem.at[2])
    lists = [
        pltpu.make_async_copy(rows_hbm, rows_ref, local_sem.at[3]),
        pltpu.make_async_copy(cols_hbm, cols_ref, local_sem.at[4]),
        pltpu.make_async_copy(counts_hbm, counts_ref, local_sem.at[5]),
    ]

    @pl.when(is_owner)
    def _():
        own_panel.start()

    for c in lists + [own_tiles, own_weight]:
        c.start()
    sums[NONE] = jnp.zeros((TILE, TILE), jnp.float32)

    def along(section):
        dz = lax.rem(z - GAP * section + ZS, ZS)
        far = jnp.where(dz <= HALF, dz, ZS - dz)
        return dz, (far + HOP - 1) // HOP

    def make_links():
        for c in lists:
            c.wait()
        keys = [along(s)[1] * SECTIONS + s for s in range(SECTIONS)]
        ranks = [sum((other < key).astype(jnp.int32) for other in keys) for key in keys]
        order = [sum(jnp.where(rank == k, s, 0) for s, rank in enumerate(ranks)) for k in range(SECTIONS)]

        def slot(i, ends):
            k, j = i // SLOTS, i % SLOTS
            section = sum(jnp.where(k == n, s, 0) for n, s in enumerate(order))
            row = jnp.where(j < counts_ref[0, section], rows_ref[0, section, j], 16)
            here = section * SLOTS + j
            before = jnp.int32(NONE)
            after = []
            for t in range(16):
                same = row == t
                before = jnp.where(same, ends[t], before)
                after.append(jnp.where(same, here, ends[t]))
            prev[here] = before
            return tuple(after)

        ends = lax.fori_loop(0, NONE, slot, (jnp.int32(NONE),) * 16)
        for t in range(16):
            last[t] = ends[t]

    def wcopy(i):
        return pltpu.make_async_remote_copy(
            weight_ref, weights.at[rep], wsend_sem.at[i], wrecv_sem.at[rep],
            device_id=(me, other(i)), device_id_type=MESH)

    def copy(section, group, b, send, recv, to, count=1):
        ref = panel.at[section, pl.ds(4 * group + b, count)]
        return pltpu.make_async_remote_copy(
            ref, ref, send_sem.at[section, send], recv_sem.at[section, recv], device_id=to, device_id_type=MESH)

    def piece(section, group, b, h, send, recv, to):
        ref = panel.at[section, 4 * group + b, pl.ds(h * (TILE // 2), TILE // 2)]
        return pltpu.make_async_remote_copy(
            ref, ref, send_sem.at[section, send + 40 * h], recv_sem.at[section, recv + 14 * h],
            device_id=to, device_id_type=MESH)

    def gets(section):
        dz, _ = along(section)
        return jnp.logical_or(dz != 0, x != 0)

    def spread(section, act, wait):
        dz, _ = along(section)
        in_row = dz == 0

        @pl.when(in_row)
        def _():
            @pl.when(x == 0)
            def _():
                for b in (0, 3, 1, 2):
                    for h in range(2):
                        for i, dx in enumerate((2, 1, 3)):
                            act(piece(section, dx, b, h, 3 * b + i, b, at(0, dx)))

            needs = {4: (0,), 3: (3, 1), 2: (2,)}
            for d in range(HOP, 0, -1):
                for h in range(2):
                    if wait and d in needs:
                        @pl.when(x != 0)
                        def _():
                            for b in needs[d]:
                                piece(section, x, b, h, 0, b, at(0, 1)).wait_recv()

                    act(piece(section, x, d % 4, h, 10 + 2 * d, 0, at(d, 0)))
                    act(piece(section, x, -d % 4, h, 11 + 2 * d, 0, at(-d, 0)))

        own = z % 4

        @pl.when(jnp.logical_not(in_row))
        def _():
            for h in range(2):
                if wait:
                    piece(section, x, own, h, 0, 0, at(1, 0)).wait_recv()

                @pl.when(dz <= HALF - HOP)
                def _():
                    act(piece(section, x, own, h, 12, 0, at(HOP, 0)))

                @pl.when(dz > HALF + HOP)
                def _():
                    act(piece(section, x, own, h, 12, 0, at(-HOP, 0)))

        out = dz <= HALF
        far = jnp.where(out, dz, ZS - dz)
        place = (far + 3) % 4
        for i in range(1, 4):
            step = (place + i) % 4 - place

            @pl.when(jnp.logical_and(far > 0, jnp.logical_or(out, far + step != HALF)))
            def _():
                act(copy(section, x, own, 27 + i, 4 + own, at(jnp.where(out, step, -step), 0)))

        @pl.when(dz == HALF)
        def _():
            for i in range(1, 4):
                act(copy(section, x, own, 30 + i, 4 + own, at(i, 0)))

    def across(section, act, wait):
        dz, _ = along(section)
        if wait:
            @pl.when(dz != 0)
            def _():
                for step in (1, 2, 3):
                    b = (z + step) % 4
                    copy(section, x, b, 0, 4 + b, at(1, 0)).wait_recv()

        for first, right, left in ((True, 0, 2), (False, 2, 0)):
            @pl.when(jnp.logical_or(dz != 0, x != 3))
            def _():
                act(copy(section, x, right, 34 if first else 38, 8 if first else 12, at(0, 1), 2))

            @pl.when(jnp.logical_or(dz != 0, x != 1))
            def _():
                act(copy(section, x, left, 35 if first else 39, 9 if first else 13, at(0, -1), 2))

    def onward(section, act, wait):
        dz, _ = along(section)
        left, right = (x + 3) % 4, (x + 1) % 4
        if wait:
            @pl.when(gets(section))
            def _():
                copy(section, left, 0, 0, 8, at(0, 1), 2).wait_recv()

        @pl.when(jnp.logical_or(dz != 0, x != 3))
        def _():
            act(copy(section, left, 0, 36, 10, at(0, 1), 2))

        if wait:
            @pl.when(gets(section))
            def _():
                copy(section, right, 2, 0, 9, at(0, 1), 2).wait_recv()

        @pl.when(jnp.logical_or(dz != 0, x != 1))
        def _():
            act(copy(section, right, 2, 37, 11, at(0, -1), 2))

    def complete(section):
        @pl.when(gets(section))
        def _():
            facing = (x + 2) % 4
            copy(section, (x + 3) % 4, 2, 0, 12, at(0, 1), 2).wait_recv()
            copy(section, (x + 1) % 4, 0, 0, 13, at(0, 1), 2).wait_recv()
            copy(section, facing, 0, 0, 10, at(0, 1), 2).wait_recv()
            copy(section, facing, 2, 0, 11, at(0, 1), 2).wait_recv()

    def products(section):
        complete(section)
        whole[...] = panel[section]
        for j in range(SLOTS):
            here = section * SLOTS + j
            sums[here] = sums[prev[here]] + jnp.dot(
                tiles[section, j], whole[cols_ref[0, section, j]], preferred_element_type=jnp.float32)

    def start(c):
        c.start()

    def step(now, carry):
        def for_each(turn, what):
            def of(section, carry):
                _, first = along(section)

                @pl.when(first == turn)
                def _():
                    what(section)

                return carry

            lax.fori_loop(0, SECTIONS, of, 0)

        for_each(now, lambda s: spread(s, start, True))

        @pl.when(now == 0)
        def _():
            def one(i, carry):
                wcopy(i).start()
                return carry

            lax.fori_loop(1, REPS, one, 0)
            make_links()
            own_tiles.wait()

        for_each(now - 1, lambda s: across(s, start, True))
        for_each(now - 2, lambda s: onward(s, start, True))
        for_each(now - 3, products)
        return carry

    pl.semaphore_wait(barrier, jnp.where(is_owner, 18, 17))

    @pl.when(is_owner)
    def _():
        own_panel.wait()

    lax.fori_loop(0, 8, step, 0)

    def bcopy(i):
        to = other(i)
        return pltpu.make_async_remote_copy(
            block_out.at[to], block_in.at[rep], bsend_sem.at[i], brecv_sem.at[rep],
            device_id=(me, to), device_id_type=MESH)

    def send_block(i, carry):
        to = other(i)
        for half in range(2):
            block_out[to, pl.ds(half * TILE, TILE), :] = sums[last[2 * to + half]].astype(jnp.bfloat16)

        bcopy(i).start()
        return carry

    lax.fori_loop(1, REPS, send_block, 0)
    for half in range(2):
        block_in[rep, pl.ds(half * TILE, TILE), :] = sums[last[2 * rep + half]].astype(jnp.bfloat16)

    own_weight.wait()

    def arrived(i, carry):
        source = other(i)
        pltpu.make_async_remote_copy(
            weight_ref, weights.at[source], wsend_sem.at[i], wrecv_sem.at[source],
            device_id=(me, source), device_id_type=MESH).wait_recv()
        pltpu.make_async_remote_copy(
            block_out.at[source], block_in.at[source], bsend_sem.at[i], brecv_sem.at[source],
            device_id=(me, source), device_id_type=MESH).wait_recv()
        return carry

    lax.fori_loop(1, REPS, arrived, 0)

    left = jnp.concatenate([block_in[i] for i in range(REPS)], axis=1)
    for q in range(REPS // 2):
        right = jnp.concatenate([weights[2 * q], weights[2 * q + 1]], axis=1)
        mixed = jnp.dot(left, right, preferred_element_type=jnp.float32)
        out_ref[:, pl.ds(2 * q * TILE, 2 * TILE)] = jnp.maximum(mixed, 0.0).astype(jnp.bfloat16)

    def finish(section, carry):
        def done(c):
            c.wait_send()

        spread(section, done, False)
        across(section, done, False)
        onward(section, done, False)
        return carry

    lax.fori_loop(0, SECTIONS, finish, 0)

    def sent(i, carry):
        wcopy(i).wait_send()
        bcopy(i).wait_send()
        return carry

    lax.fori_loop(1, REPS, sent, 0)


def shards(features, tile_rows, tile_cols, tile_counts, tile_values, weight):
    height, width = features.shape
    hbm = pl.BlockSpec(memory_space=pl.ANY)
    dma = pltpu.SemaphoreType.DMA
    return pl.pallas_call(
        kernel,
        out_shape=OUT((height // REPS, width * REPS), jnp.bfloat16),
        in_specs=[hbm] * 6,
        out_specs=pl.BlockSpec(memory_space=pltpu.VMEM),
        scratch_shapes=[
            pltpu.VMEM((SECTIONS, 16, TILE, width), jnp.bfloat16),
            pltpu.VMEM((16, TILE, width), jnp.bfloat16),
            pltpu.VMEM((SECTIONS, SLOTS, TILE, TILE), jnp.bfloat16),
            pltpu.VMEM((REPS, weight.shape[0], weight.shape[1]), jnp.bfloat16),
            pltpu.VMEM((SECTIONS * SLOTS + 1, TILE, TILE), jnp.float32),
            pltpu.VMEM((REPS, height // REPS, width), jnp.bfloat16),
            pltpu.VMEM((REPS, height // REPS, width), jnp.bfloat16),
            pltpu.SMEM(tile_rows.shape, jnp.int32),
            pltpu.SMEM(tile_cols.shape, jnp.int32),
            pltpu.SMEM(tile_counts.shape, jnp.int32),
            pltpu.SMEM((SECTIONS * SLOTS,), jnp.int32),
            pltpu.SMEM((16,), jnp.int32),
            dma((6,)),
            dma((SECTIONS, 18)),
            dma((SECTIONS, 60)),
            dma((REPS,)),
            dma((REPS,)),
            dma((REPS,)),
            dma((REPS,)),
        ],
        compiler_params=pltpu.CompilerParams(
            collective_id=0, has_side_effects=True, vmem_limit_bytes=60 << 20
        ),
        cost_estimate=pl.CostEstimate(flops=1_610_612_736, bytes_accessed=8_000_000, transcendentals=0),
        name="layer",
    )(tile_rows, tile_cols, tile_counts, features.reshape(16, TILE, width), tile_values, weight)


def solution(mesh):
    return jax.shard_map(
        shards,
        mesh=mesh,
        in_specs=(
            P("rows", "rep"),
            P("rows", None, None),
            P("rows", None, None),
            P("rows", None),
            P("rows", None, None, None, None),
            P(None, "rep"),
        ),
        out_specs=P(("rows", "rep"), None),
        check_vma=False,
    )
```
